256 devices in a mesh: dp: 8 (over x, core), latent: 32 (over z, y).
Axes of the slice: x: 4, y: 4, z: 8, core: 2. Of those that a mesh axis runs over, the one named last changes fastest.
Arguments:
- tokens: bfloat16 [4096, 8192], P('dp', 'latent'), may hold values from -6 to 6
- enc_weight: bfloat16 [8192, 8192], P('latent'), may hold values from -0.0625 to 0.0625
- dec_weight: bfloat16 [8192, 8192], P('latent'), may hold values from -0.1875 to 0.1875
- active_blocks: int32 [32, 8], P('dp'), may hold values from 0 to 63, all different within a row
- counts: int32 [4096], P('dp'), may hold values from 0 to 3
Outputs:
- grad_enc: float32 [8192, 8192], P('latent', 'dp')
- grad_dec: float32 [8192, 8192], P('latent', 'dp')
The draws below stay inside these ranges and needn't reach their ends.
Inputs may be any that keep to these rules, and one draw needn't show every extreme that they name: `active_blocks`: each row lists 8 distinct latent blocks, and every latent block is listed in some row.
All inputs are finite; a program needn't handle non-finite values.
Results may differ from the reference program's by a relative error of at most 0.02.
Values may be sent and summed in bfloat16 or wider, within the bound.
No kernel may reach another device: no remote copies, remote signals or barrier semaphores. Data moves between devices by JAX's collectives and lax.ppermute only.
A program may use at most 128 MiB of HBM per device.

```python
import jax
import jax.numpy as jnp
from jax import lax

D = 8192
BLOCK = 128
ACTIVE = 8
TOK_DEV = 512
LATENTS = 8192
LATENT_BLOCKS = 64
TOKENS = 4096
TOKEN_BLOCKS = 32


def with_ends(array, rng, least, top_value):
    spot = [jax.random.randint(jax.random.fold_in(rng, axis), (), 0, length) for axis, length in enumerate(array.shape)]
    widest = array.shape.index(max(array.shape))
    beside = spot[:widest] + [(spot[widest] + 1) % array.shape[widest]] + spot[widest + 1:]
    return array.at[tuple(spot)].set(least).at[tuple(beside)].set(top_value)


def shard_levels(rng, dims, split, least, high):
    factor_of = 1.0
    for position, shards_of in split:
        draws = jax.random.uniform(jax.random.fold_in(jax.random.fold_in(rng, 6), position), (shards_of,), jnp.float32, least / len(split), high / len(split))
        factor_of = factor_of * jnp.repeat(jnp.exp(draws), dims[position] // shards_of).reshape((-1,) + (1,) * (len(dims) - 1 - position))
    return factor_of


def choose_distinct(rng, rows, count, top, lift):
    sequence = jax.random.permutation(jax.random.fold_in(rng, 1), count)
    pull = sequence
    for power in range(3):
        pull = pull * pull // count
    pull = pull * lift // count
    tickets = jax.random.randint(jax.random.fold_in(rng, 2), (rows, count), 0, 4096) + pull
    sure = jax.random.permutation(jax.random.fold_in(rng, 3), rows)[jnp.arange(count) % rows]
    tickets = jnp.where(jnp.arange(rows)[:, None] == sure[None, :], 1 << 14, tickets)
    merit = tickets * count + jnp.arange(count)
    return lax.top_k(merit.astype(jnp.int32), top)[1].astype(jnp.int32)


def normal_values(stream_key, dims, spread, most, split=(), held_as=jnp.bfloat16):
    values = jax.random.normal(stream_key, dims, jnp.float32) * spread
    if len(split) > 0:
        values = shard_levels(stream_key, dims, split, -0.22, 0.18) * values
    return jnp.clip(values, min=-most, max=most).astype(held_as)


def setup_inputs(seed: int = 0) -> dict:
    key_list = jax.random.split(jax.random.key(seed), 6)
    tokens = normal_values(key_list[0], (TOKENS, D), 1.0, 6.0, ((0, 8), (1, 32)))
    enc_weight = normal_values(key_list[1], (LATENTS, D), D ** -0.5, 0.0625, ((0, 32),))
    dec_weight = normal_values(key_list[2], (LATENTS, D), (ACTIVE * BLOCK) ** -0.5, 0.1875, ((0, 32),))
    active_blocks = choose_distinct(key_list[3], TOKEN_BLOCKS, LATENT_BLOCKS, ACTIVE, 2048)
    counts = with_ends(jax.random.randint(key_list[4], (TOKENS,), 0, 4), jax.random.fold_in(key_list[4], 1), 0, 3).astype(jnp.int32)
    return dict(tokens=tokens, enc_weight=enc_weight, dec_weight=dec_weight, active_blocks=active_blocks, counts=counts)


def reference(tokens, enc_weight, dec_weight, active_blocks, counts):
    enc_blocks = enc_weight.reshape(LATENT_BLOCKS, BLOCK, D)
    dec_blocks = dec_weight.reshape(LATENT_BLOCKS, BLOCK, D)
    tok_blocks = tokens.reshape(TOKEN_BLOCKS, BLOCK, D)
    count_blocks = counts.reshape(TOKEN_BLOCKS, BLOCK).astype(jnp.float32)

    def one_block(args):
        rows, ids, weights = args
        w_enc = enc_blocks[ids].reshape(ACTIVE * BLOCK, D)
        w_dec = dec_blocks[ids].reshape(ACTIVE * BLOCK, D)
        pre = jnp.dot(rows, w_enc.T, preferred_element_type=jnp.float32)
        codes = pre.astype(jnp.bfloat16)
        recon = jnp.dot(codes, w_dec, preferred_element_type=jnp.float32)
        grad_out = (weights[:, None] * (recon - rows.astype(jnp.float32)) / BLOCK).astype(jnp.bfloat16)
        grad_codes = jnp.dot(grad_out, w_dec.T, preferred_element_type=jnp.float32).astype(jnp.bfloat16)
        part_dec = jnp.dot(codes.T, grad_out, preferred_element_type=jnp.float32)
        part_enc = jnp.dot(grad_codes.T, rows, preferred_element_type=jnp.float32)
        return part_dec.reshape(ACTIVE, BLOCK, D), part_enc.reshape(ACTIVE, BLOCK, D)

    part_dec, part_enc = lax.map(one_block, (tok_blocks, active_blocks, count_blocks))
    per_group = TOK_DEV // BLOCK
    groups = TOKEN_BLOCKS // per_group
    part_dec = part_dec.reshape(groups, per_group * ACTIVE, BLOCK, D)
    part_enc = part_enc.reshape(groups, per_group * ACTIVE, BLOCK, D)
    group_ids = active_blocks.reshape(groups, per_group * ACTIVE)

    def add_group(totals, args):
        ids, pdec, penc = args
        empty = jnp.zeros((LATENT_BLOCKS, BLOCK, D), jnp.float32)
        sum_dec = empty.at[ids].add(pdec).astype(jnp.bfloat16).astype(jnp.float32)
        sum_enc = empty.at[ids].add(penc).astype(jnp.bfloat16).astype(jnp.float32)
        return (totals[0] + sum_dec, totals[1] + sum_enc), None

    start = (jnp.zeros((LATENT_BLOCKS, BLOCK, D), jnp.float32), jnp.zeros((LATENT_BLOCKS, BLOCK, D), jnp.float32))
    (grad_dec, grad_enc), unused = lax.scan(add_group, start, (group_ids, part_dec, part_enc))
    return grad_enc.reshape(LATENTS, D), grad_dec.reshape(LATENTS, D)
```

```python
import functools

import jax
import jax.numpy as jnp
import numpy as np
from jax import lax
from jax.experimental import pallas as pl
from jax.experimental.pallas import tpu as pltpu
from jax.sharding import Mesh
from jax.sharding import PartitionSpec as P

BLOCK = 128
VMEM = pltpu.CompilerParams(vmem_limit_bytes=48 * 1024 * 1024)
NT = (((1,), (1,)), ((), ()))
TN = (((0,), (0,)), ((), ()))
SMEM_SPEC = pl.BlockSpec(memory_space=pltpu.SMEM)
VMEM_SPEC = pl.BlockSpec(memory_space=pltpu.VMEM)


def dot(left, right, dims):
    return lax.dot_general(left, right, dims, preferred_element_type=jnp.float32)


def pre_kernel(tb, act, ids_ref, tok_ref, enc_ref, out_ref):
    for t in range(tb):
        rows = tok_ref[t * BLOCK : (t + 1) * BLOCK, :]
        for a in range(act):
            out_ref[t * act + a] = dot(rows, enc_ref[ids_ref[t, a]], NT).astype(jnp.bfloat16)


def sum_rows(tb, act, ids_ref, codes_ref, rows_of, acc_ref, out_ref):
    acc_ref[...] = jnp.zeros_like(acc_ref)
    for t in range(tb):
        rows = rows_of(t)
        for a in range(act):
            acc_ref[ids_ref[t, a]] += dot(codes_ref[t * act + a], rows, TN)

    @pl.loop(0, acc_ref.shape[0])
    def _(b):
        out_ref[b] = acc_ref[b].astype(jnp.bfloat16)


def dec_kernel(tb, act, ids_ref, tok_ref, weight_ref, codes_ref, dec_ref, part_ref, grad_ref, acc_ref, gout_ref):
    for t in range(tb):
        here = slice(t * BLOCK, (t + 1) * BLOCK)
        recon = jnp.zeros((BLOCK, tok_ref.shape[1]), jnp.float32)
        for a in range(act):
            recon += jnp.dot(codes_ref[t * act + a], dec_ref[ids_ref[t, a]], preferred_element_type=jnp.float32)
        gout = (weight_ref[here, :] * (recon - tok_ref[here, :].astype(jnp.float32))).astype(jnp.bfloat16)
        gout_ref[here, :] = gout
        for a in range(act):
            part_ref[t * act + a] = dot(gout, dec_ref[ids_ref[t, a]], NT).astype(jnp.bfloat16)
    sum_rows(tb, act, ids_ref, codes_ref, lambda t: gout_ref[t * BLOCK : (t + 1) * BLOCK, :], acc_ref, grad_ref)


def enc_kernel(tb, act, ids_ref, tok_ref, codes_ref, grad_ref, acc_ref):
    sum_rows(tb, act, ids_ref, codes_ref, lambda t: tok_ref[t * BLOCK : (t + 1) * BLOCK, :], acc_ref, grad_ref)


def all_sum(part, axes, n):
    got = lax.all_to_all(part, axes, 0, 0, tiled=True)
    mine = jnp.sum(got.astype(jnp.float32), axis=0).astype(part.dtype)
    return lax.all_to_all(jnp.broadcast_to(mine[None], part.shape), axes, 0, 0, tiled=True)


def per_device(tokens, enc_weight, dec_weight, active_blocks, counts, *, sizes):
    nx, nc, nz, ny = (sizes[k] for k in ("x", "c", "z", "y"))
    nd = nx * nc
    feats = ("x", "c", "y")
    tok_dev, width = tokens.shape
    tb, act = active_blocks.shape
    rows = enc_weight.shape[0]
    lat_blocks = rows * nz * ny // BLOCK
    d = lax.axis_index(("x", "c"))

    swap = [(g * nz + z, z * nz + g) for g in range(nd) for z in range(nz)]
    tok = lax.ppermute(tokens, ("x", "c", "z"), swap)
    small = jnp.concatenate([counts, active_blocks.reshape(-1)])
    small = lax.ppermute(small, ("x", "c", "z"), swap)
    weights = small[:tok_dev].astype(jnp.float32)[:, None] / BLOCK
    ids = small[tok_dev:].reshape(tb, act)

    def all_rows(weight):
        mine = lax.dynamic_slice_in_dim(weight, d * (ny * width), ny * width, axis=1)
        mine = mine.reshape(rows, ny, width).transpose(1, 0, 2)
        mine = lax.all_to_all(mine, "y", 0, 0, tiled=True).reshape(ny * rows, width)
        whole = lax.all_gather(mine, "z", axis=0, tiled=True)
        return whole.reshape(lat_blocks, BLOCK, width)

    def own_rows(grad):
        part = lax.psum_scatter(grad.reshape(nz * ny * rows, width), "z", scatter_dimension=0, tiled=True)
        part = lax.all_to_all(part.reshape(ny, rows, width), "y", 0, 0, tiled=True)
        return part.transpose(1, 0, 2).reshape(rows, ny * width).astype(jnp.float32)

    enc = all_rows(enc_weight)
    dec = all_rows(dec_weight)

    pairs = jax.ShapeDtypeStruct((tb * act, BLOCK, BLOCK), jnp.bfloat16)
    grads = jax.ShapeDtypeStruct((lat_blocks, BLOCK, width), jnp.bfloat16)
    acc = pltpu.VMEM((lat_blocks, BLOCK, width), jnp.float32)

    part = pl.pallas_call(
        functools.partial(pre_kernel, tb, act),
        out_shape=pairs,
        in_specs=[SMEM_SPEC, VMEM_SPEC, VMEM_SPEC],
        out_specs=VMEM_SPEC,
        compiler_params=VMEM,
    )(ids, tok, enc)
    codes = all_sum(part, feats, nd * ny)
    part, group_dec = pl.pallas_call(
        functools.partial(dec_kernel, tb, act),
        out_shape=(pairs, grads),
        in_specs=[SMEM_SPEC] + [VMEM_SPEC] * 4,
        out_specs=(VMEM_SPEC, VMEM_SPEC),
        scratch_shapes=[acc, pltpu.VMEM((tok_dev, width), jnp.bfloat16)],
        compiler_params=VMEM,
    )(ids, tok, weights, codes, dec)
    grad_dec = own_rows(group_dec)
    grad_codes = all_sum(part, feats, nd * ny)
    group_enc = pl.pallas_call(
        functools.partial(enc_kernel, tb, act),
        out_shape=grads,
        in_specs=[SMEM_SPEC] + [VMEM_SPEC] * 2,
        out_specs=VMEM_SPEC,
        scratch_shapes=[acc],
        compiler_params=VMEM,
    )(ids, tok, grad_codes)
    grad_enc = own_rows(group_enc)
    return (grad_enc, grad_dec)


def solution(mesh):
    fine = Mesh(np.asarray(mesh.devices).reshape(4, 2, 8, 4), ("x", "c", "z", "y"))
    dp, latent = ("x", "c"), ("z", "y")
    return jax.shard_map(
        functools.partial(per_device, sizes=dict(fine.shape)),
        mesh=fine,
        in_specs=(P(dp, latent), P(latent, None), P(latent, None), P(dp, None), P(dp)),
        out_specs=(P(latent, dp), P(latent, dp)),
        check_vma=False,
    )
```

```python
import functools

import jax
import jax.numpy as jnp
import numpy as np
from jax import lax
from jax.experimental import pallas as pl
from jax.experimental.pallas import tpu as pltpu
from jax.sharding import Mesh
from jax.sharding import PartitionSpec as P

BLOCK = 128
VMEM = pltpu.CompilerParams(vmem_limit_bytes=48 * 1024 * 1024)
NT = (((1,), (1,)), ((), ()))
TN = (((0,), (0,)), ((), ()))
SMEM_SPEC = pl.BlockSpec(memory_space=pltpu.SMEM)
VMEM_SPEC = pl.BlockSpec(memory_space=pltpu.VMEM)


def dot(left, right, dims):
    return lax.dot_general(left, right, dims, preferred_element_type=jnp.float32)


def pre_kernel(tb, act, ids_ref, tok_ref, enc_ref, out_ref):
    for t in range(tb):
        rows = tok_ref[t * BLOCK : (t + 1) * BLOCK, :]
        for a in range(act):
            out_ref[t * act + a] = dot(rows, enc_ref[ids_ref[t, a]], NT).astype(jnp.bfloat16)


def sum_rows(tb, act, ids_ref, codes_ref, rows_of, acc_ref, out_ref):
    acc_ref[...] = jnp.zeros_like(acc_ref)
    for t in range(tb):
        rows = rows_of(t)
        for a in range(act):
            acc_ref[ids_ref[t, a]] += dot(codes_ref[t * act + a], rows, TN)

    @pl.loop(0, acc_ref.shape[0])
    def _(b):
        out_ref[b] = acc_ref[b].astype(jnp.bfloat16)


def dec_kernel(tb, act, ids_ref, tok_ref, weight_ref, codes_ref, dec_ref, part_ref, grad_ref, acc_ref, gout_ref):
    for t in range(tb):
        here = slice(t * BLOCK, (t + 1) * BLOCK)
        recon = jnp.zeros((BLOCK, tok_ref.shape[1]), jnp.float32)
        for a in range(act):
            recon += jnp.dot(codes_ref[t * act + a], dec_ref[ids_ref[t, a]], preferred_element_type=jnp.float32)
        gout = (weight_ref[here, :] * (recon - tok_ref[here, :].astype(jnp.float32))).astype(jnp.bfloat16)
        gout_ref[here, :] = gout
        for a in range(act):
            part_ref[t * act + a] = dot(gout, dec_ref[ids_ref[t, a]], NT).astype(jnp.bfloat16)
    sum_rows(tb, act, ids_ref, codes_ref, lambda t: gout_ref[t * BLOCK : (t + 1) * BLOCK, :], acc_ref, grad_ref)


def enc_kernel(tb, act, ids_ref, tok_ref, codes_ref, grad_ref, acc_ref):
    sum_rows(tb, act, ids_ref, codes_ref, lambda t: tok_ref[t * BLOCK : (t + 1) * BLOCK, :], acc_ref, grad_ref)


def all_sum(part, axes, n):
    got = lax.all_to_all(part, axes, 0, 0, tiled=True)
    mine = jnp.sum(got.astype(jnp.float32), axis=0).astype(part.dtype)
    return lax.all_to_all(jnp.broadcast_to(mine[None], part.shape), axes, 0, 0, tiled=True)


def per_device(tokens, enc_weight, dec_weight, active_blocks, counts, *, sizes):
    nx, nc, nz, ny = (sizes[k] for k in ("x", "c", "z", "y"))
    nd = nx * nc
    feats = ("x", "c", "y")
    tok_dev, width = tokens.shape
    tb, act = active_blocks.shape
    rows = enc_weight.shape[0]
    lat_blocks = rows * nz * ny // BLOCK
    d = lax.axis_index(("x", "c"))

    swap = [(g * nz + z, z * nz + g) for g in range(nd) for z in range(nz)]
    tok = lax.ppermute(tokens, ("x", "c", "z"), swap)
    small = jnp.concatenate([counts, active_blocks.reshape(-1)])
    small = lax.ppermute(small, ("x", "c", "z"), swap)

    def own_features(weight):
        mine = lax.dynamic_slice_in_dim(weight, d * (ny * width), ny * width, axis=1)
        mine = mine.reshape(rows, ny, width).transpose(1, 0, 2)
        return lax.all_to_all(mine, "y", 0, 0, tiled=True).reshape(ny * rows, width)

    def all_rows(mine):
        whole = lax.all_gather(mine, "z", axis=0, tiled=True)
        return whole.reshape(lat_blocks, BLOCK, width)

    def own_rows(grad):
        part = lax.psum_scatter(grad.reshape(nz * ny * rows, width), "z", scatter_dimension=0, tiled=True)
        part = lax.all_to_all(part.reshape(ny, rows, width), "y", 0, 0, tiled=True)
        return part.transpose(1, 0, 2).reshape(rows, ny * width).astype(jnp.float32)

    mine, tok, small = lax.optimization_barrier((own_features(enc_weight), tok, small))
    enc = all_rows(mine)
    dec = all_rows(own_features(dec_weight))
    weights = small[:tok_dev].astype(jnp.float32)[:, None] / BLOCK
    ids = small[tok_dev:].reshape(tb, act)

    pairs = jax.ShapeDtypeStruct((tb * act, BLOCK, BLOCK), jnp.bfloat16)
    grads = jax.ShapeDtypeStruct((lat_blocks, BLOCK, width), jnp.bfloat16)
    acc = pltpu.VMEM((lat_blocks, BLOCK, width), jnp.float32)

    part = pl.pallas_call(
        functools.partial(pre_kernel, tb, act),
        out_shape=pairs,
        in_specs=[SMEM_SPEC, VMEM_SPEC, VMEM_SPEC],
        out_specs=VMEM_SPEC,
        compiler_params=VMEM,
    )(ids, tok, enc)
    codes = all_sum(part, feats, nd * ny)
    part, group_dec = pl.pallas_call(
        functools.partial(dec_kernel, tb, act),
        out_shape=(pairs, grads),
        in_specs=[SMEM_SPEC] + [VMEM_SPEC] * 4,
        out_specs=(VMEM_SPEC, VMEM_SPEC),
        scratch_shapes=[acc, pltpu.VMEM((tok_dev, width), jnp.bfloat16)],
        compiler_params=VMEM,
    )(ids, tok, weights, codes, dec)
    grad_dec = own_rows(group_dec)
    grad_codes = all_sum(part, feats, nd * ny)
    group_enc = pl.pallas_call(
        functools.partial(enc_kernel, tb, act),
        out_shape=grads,
        in_specs=[SMEM_SPEC] + [VMEM_SPEC] * 2,
        out_specs=VMEM_SPEC,
        scratch_shapes=[acc],
        compiler_params=VMEM,
    )(ids, tok, grad_codes)
    grad_enc = own_rows(group_enc)
    return (grad_enc, grad_dec)


def solution(mesh):
    fine = Mesh(np.asarray(mesh.devices).reshape(4, 2, 8, 4), ("x", "c", "z", "y"))
    dp, latent = ("x", "c"), ("z", "y")
    return jax.shard_map(
        functools.partial(per_device, sizes=dict(fine.shape)),
        mesh=fine,
        in_specs=(P(dp, latent), P(latent, None), P(latent, None), P(dp, None), P(dp)),
        out_specs=(P(latent, dp), P(latent, dp)),
        check_vma=False,
    )
```

```python
import functools

import jax
import jax.numpy as jnp
import numpy as np
from jax import lax
from jax.experimental import pallas as pl
from jax.experimental.pallas import tpu as pltpu
from jax.sharding import Mesh
from jax.sharding import PartitionSpec as P

BLOCK = 128
VMEM = pltpu.CompilerParams(vmem_limit_bytes=48 * 1024 * 1024)
NT = (((1,), (1,)), ((), ()))
TN = (((0,), (0,)), ((), ()))
SMEM_SPEC = pl.BlockSpec(memory_space=pltpu.SMEM)
VMEM_SPEC = pl.BlockSpec(memory_space=pltpu.VMEM)


def dot(left, right, dims):
    return lax.dot_general(left, right, dims, preferred_element_type=jnp.float32)


def pre_kernel(tb, act, ids_ref, tok_ref, enc_ref, out_ref):
    for t in range(tb):
        rows = tok_ref[t * BLOCK : (t + 1) * BLOCK, :]
        for a in range(act):
            out_ref[t * act + a] = dot(rows, enc_ref[ids_ref[t, a]], NT).astype(jnp.bfloat16)


def sum_rows(tb, act, ids_ref, codes_ref, rows_of, acc_ref, out_ref):
    acc_ref[...] = jnp.zeros_like(acc_ref)
    for t in range(tb):
        rows = rows_of(t)
        for a in range(act):
            acc_ref[ids_ref[t, a]] += dot(codes_ref[t * act + a], rows, TN)

    @pl.loop(0, acc_ref.shape[0])
    def _(b):
        out_ref[b] = acc_ref[b].astype(jnp.bfloat16)


def dec_kernel(tb, act, ids_ref, tok_ref, weight_ref, codes_ref, dec_ref, part_ref, grad_ref, acc_ref, gout_ref):
    for t in range(tb):
        here = slice(t * BLOCK, (t + 1) * BLOCK)
        recon = jnp.zeros((BLOCK, tok_ref.shape[1]), jnp.float32)
        for a in range(act):
            recon += jnp.dot(codes_ref[t * act + a], dec_ref[ids_ref[t, a]], preferred_element_type=jnp.float32)
        gout = (weight_ref[here, :] * (recon - tok_ref[here, :].astype(jnp.float32))).astype(jnp.bfloat16)
        gout_ref[here, :] = gout
        for a in range(act):
            part_ref[t * act + a] = dot(gout, dec_ref[ids_ref[t, a]], NT).astype(jnp.bfloat16)
    sum_rows(tb, act, ids_ref, codes_ref, lambda t: gout_ref[t * BLOCK : (t + 1) * BLOCK, :], acc_ref, grad_ref)


def enc_kernel(tb, act, ids_ref, tok_ref, codes_ref, grad_ref, acc_ref):
    sum_rows(tb, act, ids_ref, codes_ref, lambda t: tok_ref[t * BLOCK : (t + 1) * BLOCK, :], acc_ref, grad_ref)


def all_sum(part, axes, n):
    got = lax.all_to_all(part, axes, 0, 0, tiled=True)
    mine = jnp.sum(got.astype(jnp.float32), axis=0).astype(part.dtype)
    return lax.all_to_all(jnp.broadcast_to(mine[None], part.shape), axes, 0, 0, tiled=True)


def per_device(tokens, enc_weight, dec_weight, active_blocks, counts, *, sizes):
    nx, nc, nz, ny = (sizes[k] for k in ("x", "c", "z", "y"))
    nd = nx * nc
    feats = ("x", "c", "y")
    tok_dev, width = tokens.shape
    tb, act = active_blocks.shape
    rows = enc_weight.shape[0]
    lat_blocks = rows * nz * ny // BLOCK
    d = lax.axis_index(("x", "c"))

    swap = [(g * nz + z, z * nz + g) for g in range(nd) for z in range(nz)]
    small = jnp.concatenate([counts, active_blocks.reshape(-1)])
    small = lax.ppermute(small, ("x", "c", "z"), swap)
    weights = small[:tok_dev].astype(jnp.float32)[:, None] / BLOCK
    ids = small[tok_dev:].reshape(tb, act)

    def own_features(weight):
        quarter = [
            lax.dynamic_slice_in_dim(weight, (d * ny + j) * width, width, axis=1) for j in range(ny)
        ]
        got = lax.all_to_all(jnp.stack(quarter), "y", 0, 0, tiled=True)
        return got.reshape(ny * rows, width)

    def all_rows(mine):
        whole = lax.all_gather(mine, "z", axis=0, tiled=True)
        return whole.reshape(lat_blocks, BLOCK, width)

    def own_rows(grad):
        part = lax.psum_scatter(grad.reshape(nz * ny * rows, width), "z", scatter_dimension=0, tiled=True)
        part = lax.all_to_all(part.reshape(ny, rows, width), "y", 0, 0, tiled=True)
        return jnp.concatenate([part[j] for j in range(ny)], axis=1).astype(jnp.float32)

    mine = own_features(enc_weight)
    enc = all_rows(mine)
    tokens, dec_weight, mine = lax.optimization_barrier((tokens, dec_weight, mine))
    dec = all_rows(own_features(dec_weight))
    tok = tokens.reshape(nd, tok_dev // nd, width)
    for axes in (("x", "c"), "z", ("x", "c")):
        tok = lax.all_to_all(tok, axes, 0, 0, tiled=True)
    tok = tok.reshape(tok_dev, width)

    pairs = jax.ShapeDtypeStruct((tb * act, BLOCK, BLOCK), jnp.bfloat16)
    grads = jax.ShapeDtypeStruct((lat_blocks, BLOCK, width), jnp.bfloat16)
    acc = pltpu.VMEM((lat_blocks, BLOCK, width), jnp.float32)

    part = pl.pallas_call(
        functools.partial(pre_kernel, tb, act),
        out_shape=pairs,
        in_specs=[SMEM_SPEC, VMEM_SPEC, VMEM_SPEC],
        out_specs=VMEM_SPEC,
        compiler_params=VMEM,
    )(ids, tok, enc)
    codes = all_sum(part, feats, nd * ny)
    part, group_dec = pl.pallas_call(
        functools.partial(dec_kernel, tb, act),
        out_shape=(pairs, grads),
        in_specs=[SMEM_SPEC] + [VMEM_SPEC] * 4,
        out_specs=(VMEM_SPEC, VMEM_SPEC),
        scratch_shapes=[acc, pltpu.VMEM((tok_dev, width), jnp.bfloat16)],
        compiler_params=VMEM,
    )(ids, tok, weights, codes, dec)
    grad_dec = own_rows(group_dec)
    grad_codes = all_sum(part, feats, nd * ny)
    group_enc = pl.pallas_call(
        functools.partial(enc_kernel, tb, act),
        out_shape=grads,
        in_specs=[SMEM_SPEC] + [VMEM_SPEC] * 2,
        out_specs=VMEM_SPEC,
        scratch_shapes=[acc],
        compiler_params=VMEM,
    )(ids, tok, grad_codes)
    grad_enc = own_rows(group_enc)
    return (grad_enc, grad_dec)


def solution(mesh):
    fine = Mesh(np.asarray(mesh.devices).reshape(4, 2, 8, 4), ("x", "c", "z", "y"))
    dp, latent = ("x", "c"), ("z", "y")
    return jax.shard_map(
        functools.partial(per_device, sizes=dict(fine.shape)),
        mesh=fine,
        in_specs=(P(dp, latent), P(latent, None), P(latent, None), P(dp, None), P(dp)),
        out_specs=(P(latent, dp), P(latent, dp)),
        check_vma=False,
    )
```

```python
import functools

import jax
import jax.numpy as jnp
import numpy as np
from jax import lax
from jax.experimental import pallas as pl
from jax.experimental.pallas import tpu as pltpu
from jax.sharding import Mesh
from jax.sharding import PartitionSpec as P

BLOCK = 128
VMEM = pltpu.CompilerParams(vmem_limit_bytes=48 * 1024 * 1024)
ALL_VMEM = pltpu.CompilerParams(vmem_limit_bytes=61 * 1024 * 1024)
NT = (((1,), (1,)), ((), ()))
TN = (((0,), (0,)), ((), ()))
SMEM_SPEC = pl.BlockSpec(memory_space=pltpu.SMEM)
VMEM_SPEC = pl.BlockSpec(memory_space=pltpu.VMEM)


def dot(left, right, dims):
    return lax.dot_general(left, right, dims, preferred_element_type=jnp.float32)


def split_kernel(ny, sub, d_ref, *refs):
    out_ref = refs[-1]
    for z, in_ref in enumerate(refs[:-1]):
        for y in range(ny):
            for i in range(in_ref.shape[0] // BLOCK):
                at = i * BLOCK + y * sub
                out_ref[z * ny + y, i] = in_ref[at : at + sub, :]


def select(ids_ref, weight_ref, t, act, sel_ref):
    pieces, _, sub, lanes = weight_ref.shape
    for a in range(act):
        for p in range(pieces):
            sel_ref[t, a * sub : (a + 1) * sub, p * lanes : (p + 1) * lanes] = weight_ref[p, ids_ref[t, a]]


def token_rows(tok_ref, at):
    return jnp.concatenate([tok_ref[q, at, :] for q in range(tok_ref.shape[0])], axis=1)


def block(t):
    return slice(t * BLOCK, (t + 1) * BLOCK)


def pre_kernel(tb, act, ids_ref, tok_ref, enc_ref, out_ref, sel_ref):
    for t in range(tb):
        select(ids_ref, enc_ref, t, act, sel_ref)
        out_ref[block(t), :] = dot(token_rows(tok_ref, block(t)), sel_ref[t], NT).astype(jnp.bfloat16)


def recon_kernel(tb, act, ids_ref, codes_ref, dec_ref, out_ref, sel_ref):
    for t in range(tb):
        select(ids_ref, dec_ref, t, act, sel_ref)
        out_ref[t] = jnp.dot(
            codes_ref[block(t), :], sel_ref[t], preferred_element_type=jnp.float32
        ).astype(jnp.bfloat16)


def error_kernel(y_ref, tok_ref, weight_ref, recon_ref, out_ref):
    at = pl.ds(pl.multiple_of(y_ref[0] * BLOCK, BLOCK), BLOCK)
    recon = recon_ref[0].astype(jnp.float32)
    for k in range(1, recon_ref.shape[0]):
        recon += recon_ref[k].astype(jnp.float32)
    gout = weight_ref[at, :] * (recon - token_rows(tok_ref, at).astype(jnp.float32))
    gout = gout.astype(jnp.bfloat16)
    for k in range(out_ref.shape[0]):
        out_ref[k] = gout


def sum_rows(tb, act, ids_ref, codes_ref, rows_of, prod_ref, acc_ref, out_ref):
    pieces, blocks, sub, lanes = acc_ref.shape
    acc_ref[...] = jnp.zeros_like(acc_ref)
    for t in range(tb):
        prod_ref[...] = dot(codes_ref[block(t), :], rows_of(t), TN)
        for a in range(act):
            for p in range(pieces):
                acc_ref[p, ids_ref[t, a]] += prod_ref[a * sub : (a + 1) * sub, p * lanes : (p + 1) * lanes]

    @pl.loop(0, blocks)
    def _(b):
        for p in range(pieces):
            out_ref[p, b] = acc_ref[p, b].astype(jnp.bfloat16)


def dec_kernel(tb, act, ids_ref, codes_ref, gout_ref, sel_ref, part_ref, grad_ref, prod_ref, acc_ref):
    for t in range(tb):
        part_ref[block(t), :] = dot(gout_ref[t], sel_ref[t], NT).astype(jnp.bfloat16)
    sum_rows(tb, act, ids_ref, codes_ref, lambda t: gout_ref[t], prod_ref, acc_ref, grad_ref)


def enc_kernel(tb, act, ids_ref, codes_ref, tok_ref, grad_ref, prod_ref, acc_ref):
    sum_rows(tb, act, ids_ref, codes_ref, lambda t: token_rows(tok_ref, block(t)), prod_ref, acc_ref, grad_ref)


def join_kernel(in_ref, out_ref):
    pieces, ny, blocks, sub, lanes = in_ref.shape
    for p in range(pieces):
        for y in range(ny):
            for i in range(blocks):
                at = i * BLOCK + y * sub
                out_ref[at : at + sub, p * lanes : (p + 1) * lanes] = in_ref[p, y, i].astype(jnp.float32)


def call(kernel, out_shape, n_smem, n_vmem, scratch=()):
    many = isinstance(out_shape, tuple)
    return pl.pallas_call(
        kernel,
        out_shape=out_shape,
        in_specs=[SMEM_SPEC] * n_smem + [VMEM_SPEC] * n_vmem,
        out_specs=(VMEM_SPEC,) * len(out_shape) if many else VMEM_SPEC,
        scratch_shapes=list(scratch),
        compiler_params=VMEM,
    )


def all_sum(part, axis, n):
    got = lax.all_to_all(part.reshape(n, -1, part.shape[1]), axis, 0, 0, tiled=True)
    mine = jnp.sum(got.astype(jnp.float32), axis=0).astype(part.dtype)
    got = lax.all_to_all(jnp.broadcast_to(mine[None], got.shape), axis, 0, 0, tiled=True)
    return got.reshape(part.shape)


def per_device(tokens, enc_weight, dec_weight, active_blocks, counts, *, sizes):
    nd, nz, ny = sizes["x"] * sizes["c"], sizes["z"], sizes["y"]
    dp, latent = ("x", "c"), ("z", "y")
    tok_dev, width = tokens.shape
    tb, act = active_blocks.shape
    rows, model = enc_weight.shape
    feats = model // nz
    lanes = feats // nd
    sub = BLOCK // ny
    mine_blocks = rows // BLOCK
    blocks = nz * ny * mine_blocks
    d = lax.axis_index(dp).astype(jnp.int32).reshape(1)
    y = lax.axis_index("y").astype(jnp.int32).reshape(1)
    weights = counts.astype(jnp.float32)[:, None] / BLOCK

    def spread(weight):
        out = (nz * ny, mine_blocks, sub, lanes)
        pieces = pl.pallas_call(
            functools.partial(split_kernel, ny, sub),
            out_shape=jax.ShapeDtypeStruct(out, jnp.bfloat16),
            grid_spec=pltpu.PrefetchScalarGridSpec(
                num_scalar_prefetch=1,
                grid=(1,),
                in_specs=[
                    pl.BlockSpec((rows, lanes), lambda i, d_ref, z=z: (0, z * nd + d_ref[0]))
                    for z in range(nz)
                ],
                out_specs=pl.BlockSpec(out, lambda i, d_ref: (0, 0, 0, 0)),
            ),
            compiler_params=ALL_VMEM,
        )(d, *[weight] * nz)
        return lax.all_to_all(pieces, latent, 0, 0, tiled=True)

    def gather(pieces):
        whole = lax.all_gather(pieces.reshape(blocks * sub, lanes), dp, axis=0, tiled=True)
        return whole.reshape(nd, blocks, sub, lanes)

    def own(grad):
        part = lax.psum_scatter(grad.reshape(nd * blocks * sub, lanes), dp, scatter_dimension=0, tiled=True)
        part = lax.all_to_all(part.reshape(nz * ny, mine_blocks, sub, lanes), latent, 0, 0, tiled=True)
        part = lax.all_to_all(part.reshape(nz, ny, mine_blocks, sub, lanes), dp, 0, 0, tiled=True)
        return call(join_kernel, jax.ShapeDtypeStruct((rows, nd * lanes), jnp.float32), 0, 1)(part)

    mine = spread(enc_weight)
    enc = gather(mine)
    tokens, dec_weight, mine = lax.optimization_barrier((tokens, dec_weight, mine))
    dec = gather(spread(dec_weight))
    tok = lax.all_to_all(jnp.broadcast_to(tokens[None], (ny, tok_dev, width)), "y", 0, 0, tiled=True)

    half = jnp.bfloat16
    codes_like = jax.ShapeDtypeStruct((tok_dev, act * sub), half)
    sel_like = jax.ShapeDtypeStruct((tb, act * sub, feats), half)
    rows_like = jax.ShapeDtypeStruct((tb, BLOCK, feats), half)
    grad_like = jax.ShapeDtypeStruct((nd, blocks, sub, lanes), half)
    sums = (pltpu.VMEM((act * sub, feats), jnp.float32), pltpu.VMEM((nd, blocks, sub, lanes), jnp.float32))

    part = call(
        functools.partial(pre_kernel, tb, act), codes_like, 1, 2, [pltpu.VMEM(sel_like.shape, half)]
    )(active_blocks, tok, enc)
    codes = all_sum(part, "z", nz)
    recon, sel = call(functools.partial(recon_kernel, tb, act), (rows_like, sel_like), 1, 2)(
        active_blocks, codes, dec
    )
    recon = lax.all_to_all(recon, "y", 0, 0, tiled=True)
    gout = call(error_kernel, rows_like, 1, 3)(y, tok, weights, recon)
    gout = lax.all_to_all(gout, "y", 0, 0, tiled=True)
    part, group_dec = call(functools.partial(dec_kernel, tb, act), (codes_like, grad_like), 1, 3, sums)(
        active_blocks, codes, gout, sel
    )
    grad_dec = own(group_dec)
    grad_codes = all_sum(part, "z", nz)
    group_enc = call(functools.partial(enc_kernel, tb, act), grad_like, 1, 2, sums)(
        active_blocks, grad_codes, tok
    )
    grad_enc = own(group_enc)
    return (grad_enc, grad_dec)


def solution(mesh):
    fine = Mesh(np.asarray(mesh.devices).reshape(4, 2, 8, 4), ("x", "c", "z", "y"))
    dp, latent = ("x", "c"), ("z", "y")
    return jax.shard_map(
        functools.partial(per_device, sizes=dict(fine.shape)),
        mesh=fine,
        in_specs=(P(dp, latent), P(latent, None), P(latent, None), P(dp, None), P(dp)),
        out_specs=(P(latent, dp), P(latent, dp)),
        check_vma=False,
    )
```

```python
import functools

import jax
import jax.numpy as jnp
import numpy as np
from jax import lax
from jax.experimental import pallas as pl
from jax.experimental.pallas import tpu as pltpu
from jax.sharding import Mesh
from jax.sharding import PartitionSpec as P

BLOCK = 128
VMEM = pltpu.CompilerParams(vmem_limit_bytes=48 * 1024 * 1024)
ALL_VMEM = pltpu.CompilerParams(vmem_limit_bytes=61 * 1024 * 1024)
NT = (((1,), (1,)), ((), ()))
TN = (((0,), (0,)), ((), ()))
SMEM_SPEC = pl.BlockSpec(memory_space=pltpu.SMEM)
VMEM_SPEC = pl.BlockSpec(memory_space=pltpu.VMEM)


def dot(left, right, dims):
    return lax.dot_general(left, right, dims, preferred_element_type=jnp.float32)


def split_kernel(nh, nl, ny, sub, lanes, d_ref, in_ref, out_ref):
    for h in range(nh):
        for l in range(nl):
            for i in range(in_ref.shape[0] // BLOCK):
                at = i * BLOCK + h * sub
                for q in range(ny):
                    col = (q * nl + l) * lanes
                    out_ref[h * nl + l, i, :, q * lanes : (q + 1) * lanes] = in_ref[at : at + sub, col : col + lanes]


def select(ids_ref, weight_ref, t, act, sel_ref):
    pieces, _, sub, lanes = weight_ref.shape
    for a in range(act):
        for p in range(pieces):
            sel_ref[t, a * sub : (a + 1) * sub, p * lanes : (p + 1) * lanes] = weight_ref[p, ids_ref[t, a]]


def token_rows(tok_ref, at):
    quarters, pieces = tok_ref.shape[:2]
    return jnp.concatenate([tok_ref[q, p, at, :] for p in range(pieces) for q in range(quarters)], axis=1)


def block(t):
    return slice(t * BLOCK, (t + 1) * BLOCK)


def pre_kernel(tb, act, ids_ref, tok_ref, enc_ref, out_ref, sel_ref):
    for t in range(tb):
        select(ids_ref, enc_ref, t, act, sel_ref)
        out_ref[block(t), :] = dot(token_rows(tok_ref, block(t)), sel_ref[t], NT).astype(jnp.bfloat16)


def recon_kernel(tb, act, ids_ref, codes_ref, dec_ref, out_ref, sel_ref):
    for t in range(tb):
        select(ids_ref, dec_ref, t, act, sel_ref)
        out_ref[t] = jnp.dot(
            codes_ref[block(t), :], sel_ref[t], preferred_element_type=jnp.float32
        ).astype(jnp.bfloat16)


def error_kernel(mine_ref, tok_ref, weight_ref, recon_ref, out_ref):
    at = pl.ds(pl.multiple_of(mine_ref[0] * BLOCK, BLOCK), BLOCK)
    recon = recon_ref[0].astype(jnp.float32)
    for k in range(1, recon_ref.shape[0]):
        recon += recon_ref[k].astype(jnp.float32)
    gout = weight_ref[at, :] * (recon - token_rows(tok_ref, at).astype(jnp.float32))
    gout = gout.astype(jnp.bfloat16)
    for k in range(out_ref.shape[0]):
        out_ref[k] = gout


def sum_rows(tb, act, ids_ref, codes_ref, rows_of, prod_ref, acc_ref, out_ref):
    pieces, blocks, sub, lanes = acc_ref.shape
    acc_ref[...] = jnp.zeros_like(acc_ref)
    for t in range(tb):
        prod_ref[...] = dot(codes_ref[block(t), :], rows_of(t), TN)
        for a in range(act):
            for p in range(pieces):
                acc_ref[p, ids_ref[t, a]] += prod_ref[a * sub : (a + 1) * sub, p * lanes : (p + 1) * lanes]

    @pl.loop(0, blocks)
    def _(b):
        for p in range(pieces):
            out_ref[p, b] = acc_ref[p, b].astype(jnp.bfloat16)


def dec_kernel(tb, act, ids_ref, codes_ref, gout_ref, sel_ref, part_ref, grad_ref, prod_ref, acc_ref):
    for t in range(tb):
        part_ref[block(t), :] = dot(gout_ref[t], sel_ref[t], NT).astype(jnp.bfloat16)
    sum_rows(tb, act, ids_ref, codes_ref, lambda t: gout_ref[t], prod_ref, acc_ref, grad_ref)


def enc_kernel(tb, act, ids_ref, codes_ref, tok_ref, grad_ref, prod_ref, acc_ref):
    sum_rows(tb, act, ids_ref, codes_ref, lambda t: token_rows(tok_ref, block(t)), prod_ref, acc_ref, grad_ref)


def join_kernel(nh, nl, ny, lanes, in_ref, out_ref):
    _, blocks, sub, _ = in_ref.shape
    for h in range(nh):
        for l in range(nl):
            for i in range(blocks):
                at = i * BLOCK + h * sub
                for q in range(ny):
                    col = (q * nl + l) * lanes
                    part = in_ref[h * nl + l, i, :, q * lanes : (q + 1) * lanes]
                    out_ref[at : at + sub, col : col + lanes] = part.astype(jnp.float32)


def call(kernel, out_shape, n_smem, n_vmem, scratch=()):
    many = isinstance(out_shape, tuple)
    return pl.pallas_call(
        kernel,
        out_shape=out_shape,
        in_specs=[SMEM_SPEC] * n_smem + [VMEM_SPEC] * n_vmem,
        out_specs=(VMEM_SPEC,) * len(out_shape) if many else VMEM_SPEC,
        scratch_shapes=list(scratch),
        compiler_params=VMEM,
    )


def all_sum(part, axis, n):
    got = lax.all_to_all(part.reshape(n, -1, part.shape[1]), axis, 0, 0, tiled=True)
    mine = jnp.sum(got.astype(jnp.float32), axis=0).astype(part.dtype)
    got = lax.all_to_all(jnp.broadcast_to(mine[None], got.shape), axis, 0, 0, tiled=True)
    return got.reshape(part.shape)


def per_device(tokens, enc_weight, dec_weight, active_blocks, counts, *, sizes):
    nx, nc, nh, nl, ny = (sizes[k] for k in ("x", "c", "h", "l", "y"))
    group, feat, inner = ("c", "y"), ("x", "l"), ("h", "l")
    tok_dev, width = tokens.shape
    tb, act = active_blocks.shape
    rows, model = enc_weight.shape
    feats = model // (nx * nl)
    lanes = width // nl
    cols = feats // nc
    sub = BLOCK // nh
    own_blocks = rows // BLOCK
    blocks = nh * nl * ny * own_blocks
    d = lax.axis_index(("x", "c")).astype(jnp.int32).reshape(1)
    h = lax.axis_index("h").astype(jnp.int32).reshape(1)

    def spread(weight):
        out = (nh * nl, own_blocks, sub, cols)
        pieces = pl.pallas_call(
            functools.partial(split_kernel, nh, nl, ny, sub, lanes),
            out_shape=jax.ShapeDtypeStruct(out, jnp.bfloat16),
            grid_spec=pltpu.PrefetchScalarGridSpec(
                num_scalar_prefetch=1,
                grid=(1,),
                in_specs=[pl.BlockSpec((rows, nc * cols), lambda i, d_ref: (0, d_ref[0]))],
                out_specs=pl.BlockSpec(out, lambda i, d_ref: (0, 0, 0, 0)),
            ),
            compiler_params=ALL_VMEM,
        )(d, weight)
        return lax.all_to_all(pieces, inner, 0, 0, tiled=True)

    def gather(pieces):
        whole = lax.all_gather(pieces.reshape(-1, cols), group, axis=0, tiled=True)
        return whole.reshape(nc, blocks, sub, cols)

    def own(grad):
        part = lax.psum_scatter(grad.reshape(-1, cols), group, scatter_dimension=0, tiled=True)
        part = lax.all_to_all(part.reshape(nh * nl, own_blocks, sub, cols), inner, 0, 0, tiled=True)
        return call(
            functools.partial(join_kernel, nh, nl, ny, lanes),
            jax.ShapeDtypeStruct((rows, nc * cols), jnp.float32),
            0,
            1,
        )(part)

    swap = [
        ((x * nh + g) * ny + q, (g * nh + q) * ny + x) for x in range(nx) for g in range(nh) for q in range(ny)
    ]
    small = jnp.concatenate([counts, active_blocks.reshape(-1)])
    small = lax.ppermute(small, ("x", "h", "y"), swap)
    tokens = lax.ppermute(tokens, ("x", "h", "y"), swap)
    mine, tokens, small = lax.optimization_barrier((spread(enc_weight), tokens, small))
    enc = gather(mine)
    dec_weight, tokens, mine = lax.optimization_barrier((dec_weight, tokens, mine))
    dec = gather(spread(dec_weight))
    weights = small[:tok_dev].astype(jnp.float32)[:, None] / BLOCK
    ids = small[tok_dev:].reshape(tb, act)
    ids = (ids // own_blocks % ny * (nh * nl) + ids // (own_blocks * ny)) * own_blocks + ids % own_blocks
    parts = jnp.stack([tokens[:, l * lanes : (l + 1) * lanes] for l in range(nl)])
    parts = jnp.broadcast_to(parts[None], (nh, *parts.shape)).reshape(nh * nl, tok_dev, lanes)
    tok = lax.all_to_all(parts, inner, 0, 0, tiled=True).reshape(nh, nl, tok_dev, lanes)

    half = jnp.bfloat16
    codes_like = jax.ShapeDtypeStruct((tok_dev, act * sub), half)
    sel_like = jax.ShapeDtypeStruct((tb, act * sub, feats), half)
    rows_like = jax.ShapeDtypeStruct((tb, BLOCK, feats), half)
    grad_like = jax.ShapeDtypeStruct((nc, blocks, sub, cols), half)
    sums = (pltpu.VMEM((act * sub, feats), jnp.float32), pltpu.VMEM((nc, blocks, sub, cols), jnp.float32))

    part = call(
        functools.partial(pre_kernel, tb, act), codes_like, 1, 2, [pltpu.VMEM(sel_like.shape, half)]
    )(ids, tok, enc)
    codes = all_sum(part, feat, nx * nl)
    recon, sel = call(functools.partial(recon_kernel, tb, act), (rows_like, sel_like), 1, 2)(
        ids, codes, dec
    )
    recon = lax.all_to_all(recon, "h", 0, 0, tiled=True)
    gout = call(error_kernel, rows_like, 1, 3)(h, tok, weights, recon)
    gout = lax.all_to_all(gout, "h", 0, 0, tiled=True)
    part, group_dec = call(functools.partial(dec_kernel, tb, act), (codes_like, grad_like), 1, 3, sums)(
        ids, codes, gout, sel
    )
    grad_dec = own(group_dec)
    grad_codes = all_sum(part, feat, nx * nl)
    group_enc = call(functools.partial(enc_kernel, tb, act), grad_like, 1, 2, sums)(
        ids, grad_codes, tok
    )
    grad_enc = own(group_enc)
    return (grad_enc, grad_dec)


def solution(mesh):
    fine = Mesh(np.asarray(mesh.devices).reshape(4, 2, 4, 2, 4), ("x", "c", "h", "l", "y"))
    dp, latent = ("x", "c"), ("h", "l", "y")
    return jax.shard_map(
        functools.partial(per_device, sizes=dict(fine.shape)),
        mesh=fine,
        in_specs=(P(dp, latent), P(latent, None), P(latent, None), P(dp, None), P(dp)),
        out_specs=(P(latent, dp), P(latent, dp)),
        check_vma=False,
    )
```

```python
import functools

import jax
import jax.numpy as jnp
import numpy as np
from jax import lax
from jax.experimental import pallas as pl
from jax.experimental.pallas import tpu as pltpu
from jax.sharding import Mesh
from jax.sharding import PartitionSpec as P

BLOCK = 128
VMEM = pltpu.CompilerParams(vmem_limit_bytes=48 * 1024 * 1024)
MOST_VMEM = pltpu.CompilerParams(vmem_limit_bytes=61 * 1024 * 1024)
NT = (((1,), (1,)), ((), ()))
TN = (((0,), (0,)), ((), ()))
SMEM_SPEC = pl.BlockSpec(memory_space=pltpu.SMEM)
VMEM_SPEC = pl.BlockSpec(memory_space=pltpu.VMEM)
HBM_SPEC = pl.BlockSpec(memory_space=pltpu.HBM)
PIECES = 8


def dot(left, right, dims):
    return lax.dot_general(left, right, dims, preferred_element_type=jnp.float32)


def fetch(tb, act, ids_ref, weight_ref, got_ref, sem):
    copies = [
        pltpu.make_async_copy(weight_ref.at[ids_ref[t, a]], got_ref.at[t * act + a], sem.at[t * act + a])
        for t in range(tb)
        for a in range(act)
    ]
    for copy in copies:
        copy.start()
    return lambda pair: copies[pair].wait()


def pre_kernel(tb, act, ids_ref, tok_ref, enc_ref, out_ref, got_ref, sem):
    wait = fetch(tb, act, ids_ref, enc_ref, got_ref, sem)
    for t in range(tb):
        rows = tok_ref[t * BLOCK : (t + 1) * BLOCK, :]
        for a in range(act):
            pair = t * act + a
            wait(pair)
            out_ref[pair] = dot(rows, got_ref[pair], NT).astype(jnp.bfloat16)


def add_rows(t, act, ids_ref, codes_ref, rows, acc_ref):
    for a in range(act):
        acc_ref[ids_ref[t, a]] += dot(codes_ref[t * act + a], rows, TN)


def put(acc_ref, half_ref, out_ref, sem):
    step = acc_ref.shape[0] // PIECES
    copies = []
    for k in range(PIECES):
        for b in range(k * step, (k + 1) * step):
            half_ref[b] = acc_ref[b].astype(jnp.bfloat16)
        here = pl.ds(k * step, step)
        copies.append(pltpu.make_async_copy(half_ref.at[here], out_ref.at[here], sem.at[k]))
        copies[-1].start()
    for copy in copies:
        copy.wait()


def dec_kernel(
    tb, act, ids_ref, tok_ref, weight_ref, codes_ref, dec_ref, part_ref, grad_ref, acc_ref, half_ref, got_ref, in_sem, out_sem
):
    wait = fetch(tb, act, ids_ref, dec_ref, got_ref, in_sem)
    acc_ref[...] = jnp.zeros_like(acc_ref)
    for t in range(tb):
        here = slice(t * BLOCK, (t + 1) * BLOCK)
        recon = jnp.zeros((BLOCK, tok_ref.shape[1]), jnp.float32)
        for a in range(act):
            wait(t * act + a)
            recon += jnp.dot(codes_ref[t * act + a], got_ref[t * act + a], preferred_element_type=jnp.float32)
        gout = (weight_ref[here, :] * (recon - tok_ref[here, :].astype(jnp.float32))).astype(jnp.bfloat16)
        add_rows(t, act, ids_ref, codes_ref, gout, acc_ref)
        for a in range(act):
            part_ref[t * act + a] = dot(gout, got_ref[t * act + a], NT).astype(jnp.bfloat16)
    put(acc_ref, half_ref, grad_ref, out_sem)


def enc_kernel(tb, act, ids_ref, tok_ref, codes_ref, grad_ref, acc_ref, half_ref, out_sem):
    acc_ref[...] = jnp.zeros_like(acc_ref)
    for t in range(tb):
        add_rows(t, act, ids_ref, codes_ref, tok_ref[t * BLOCK : (t + 1) * BLOCK, :], acc_ref)
    put(acc_ref, half_ref, grad_ref, out_sem)


def all_sum(part, axes, n):
    got = lax.all_to_all(part, axes, 0, 0, tiled=True)
    mine = jnp.sum(got.astype(jnp.float32), axis=0).astype(part.dtype)
    return lax.all_to_all(jnp.broadcast_to(mine[None], part.shape), axes, 0, 0, tiled=True)


def per_device(tokens, enc_weight, dec_weight, active_blocks, counts, *, sizes):
    nx, nc, nz, ny = (sizes[k] for k in ("x", "c", "z", "y"))
    nd = nx * nc
    feats = ("x", "c", "y")
    tok_dev, width = tokens.shape
    tb, act = active_blocks.shape
    rows = enc_weight.shape[0]
    lat_blocks = rows * nz * ny // BLOCK
    d = lax.axis_index(("x", "c"))

    swap = [(g * nz + z, z * nz + g) for g in range(nd) for z in range(nz)]
    small = jnp.concatenate([counts, active_blocks.reshape(-1)])
    small = lax.ppermute(small, ("x", "c", "z"), swap)
    weights = small[:tok_dev].astype(jnp.float32)[:, None] / BLOCK
    ids = small[tok_dev:].reshape(tb, act)

    def own_features(weight):
        quarter = [
            lax.dynamic_slice_in_dim(weight, (d * ny + j) * width, width, axis=1) for j in range(ny)
        ]
        got = lax.all_to_all(jnp.stack(quarter), "y", 0, 0, tiled=True)
        return got.reshape(ny * rows, width)

    def all_rows(mine):
        whole = lax.all_gather(mine, "z", axis=0, tiled=True)
        return whole.reshape(lat_blocks, BLOCK, width)

    def own_rows(grad):
        part = lax.psum_scatter(grad.reshape(nz * ny * rows, width), "z", scatter_dimension=0, tiled=True)
        part = lax.all_to_all(part.reshape(ny, rows, width), "y", 0, 0, tiled=True)
        return jnp.concatenate([part[j] for j in range(ny)], axis=1).astype(jnp.float32)

    mine = own_features(enc_weight)
    enc = all_rows(mine)
    tokens, dec_weight, mine = lax.optimization_barrier((tokens, dec_weight, mine))
    dec = all_rows(own_features(dec_weight))
    tok = tokens.reshape(nd, tok_dev // nd, width)
    for axes in (("x", "c"), "z", ("x", "c")):
        tok = lax.all_to_all(tok, axes, 0, 0, tiled=True)
    tok = tok.reshape(tok_dev, width)

    pairs = jax.ShapeDtypeStruct((tb * act, BLOCK, BLOCK), jnp.bfloat16)
    grads = jax.ShapeDtypeStruct((lat_blocks, BLOCK, width), jnp.bfloat16)
    acc = [pltpu.VMEM(grads.shape, jnp.float32), pltpu.VMEM(grads.shape, jnp.bfloat16)]
    got = pltpu.VMEM((tb * act, BLOCK, width), jnp.bfloat16)
    in_sem, out_sem = pltpu.SemaphoreType.DMA((tb * act,)), pltpu.SemaphoreType.DMA((PIECES,))

    part = pl.pallas_call(
        functools.partial(pre_kernel, tb, act),
        out_shape=pairs,
        in_specs=[SMEM_SPEC, VMEM_SPEC, HBM_SPEC],
        out_specs=VMEM_SPEC,
        scratch_shapes=[got, in_sem],
        compiler_params=MOST_VMEM,
    )(ids, tok, enc)
    codes = all_sum(part, feats, nd * ny)
    part, group_dec = pl.pallas_call(
        functools.partial(dec_kernel, tb, act),
        out_shape=(pairs, grads),
        in_specs=[SMEM_SPEC] + [VMEM_SPEC] * 3 + [HBM_SPEC],
        out_specs=(VMEM_SPEC, HBM_SPEC),
        scratch_shapes=acc + [got, in_sem, out_sem],
        compiler_params=VMEM,
    )(ids, tok, weights, codes, dec)
    grad_dec = own_rows(group_dec)
    grad_codes = all_sum(part, feats, nd * ny)
    group_enc = pl.pallas_call(
        functools.partial(enc_kernel, tb, act),
        out_shape=grads,
        in_specs=[SMEM_SPEC] + [VMEM_SPEC] * 2,
        out_specs=HBM_SPEC,
        scratch_shapes=acc + [out_sem],
        compiler_params=MOST_VMEM,
    )(ids, tok, grad_codes)
    grad_enc = own_rows(group_enc)
    return (grad_enc, grad_dec)


def solution(mesh):
    fine = Mesh(np.asarray(mesh.devices).reshape(4, 2, 8, 4), ("x", "c", "z", "y"))
    dp, latent = ("x", "c"), ("z", "y")
    return jax.shard_map(
        functools.partial(per_device, sizes=dict(fine.shape)),
        mesh=fine,
        in_specs=(P(dp, latent), P(latent, None), P(latent, None), P(dp, None), P(dp)),
        out_specs=(P(latent, dp), P(latent, dp)),
        check_vma=False,
    )
```

```python
import functools

import jax
import jax.numpy as jnp
import numpy as np
from jax import lax
from jax.experimental import pallas as pl
from jax.experimental.pallas import tpu as pltpu
from jax.sharding import Mesh
from jax.sharding import PartitionSpec as P

BLOCK = 128
VMEM = pltpu.CompilerParams(vmem_limit_bytes=48 * 1024 * 1024)
NT = (((1,), (1,)), ((), ()))
TN = (((0,), (0,)), ((), ()))
SMEM_SPEC = pl.BlockSpec(memory_space=pltpu.SMEM)
VMEM_SPEC = pl.BlockSpec(memory_space=pltpu.VMEM)
HBM_SPEC = pl.BlockSpec(memory_space=pltpu.HBM)
PIECES = 8


def dot(left, right, dims):
    return lax.dot_general(left, right, dims, preferred_element_type=jnp.float32)


def pre_kernel(tb, act, ids_ref, tok_ref, enc_ref, out_ref):
    for t in range(tb):
        rows = tok_ref[t * BLOCK : (t + 1) * BLOCK, :]
        for a in range(act):
            out_ref[t * act + a] = dot(rows, enc_ref[ids_ref[t, a]], NT).astype(jnp.bfloat16)


def sum_rows(tb, act, ids_ref, codes_ref, rows_of, acc_ref, out_ref):
    acc_ref[...] = jnp.zeros_like(acc_ref)
    for t in range(tb):
        rows = rows_of(t)
        for a in range(act):
            acc_ref[ids_ref[t, a]] += dot(codes_ref[t * act + a], rows, TN)

    @pl.loop(0, acc_ref.shape[0])
    def _(b):
        out_ref[b] = acc_ref[b].astype(jnp.bfloat16)


def put(acc_ref, half_ref, out_ref, sem):
    step = acc_ref.shape[0] // PIECES
    copies = []
    for k in range(PIECES):
        for b in range(k * step, (k + 1) * step):
            half_ref[b] = acc_ref[b].astype(jnp.bfloat16)
        here = pl.ds(k * step, step)
        copies.append(pltpu.make_async_copy(half_ref.at[here], out_ref.at[here], sem.at[k]))
        copies[-1].start()
    for copy in copies:
        copy.wait()


def dec_kernel(
    tb, act, ids_ref, tok_ref, weight_ref, codes_ref, dec_ref, part_ref, grad_ref, acc_ref, half_ref, got_ref, in_sem, out_sem
):
    copy = pltpu.make_async_copy(dec_ref, got_ref, in_sem)
    copy.start()
    acc_ref[...] = jnp.zeros_like(acc_ref)
    copy.wait()
    for t in range(tb):
        here = slice(t * BLOCK, (t + 1) * BLOCK)
        recon = jnp.zeros((BLOCK, tok_ref.shape[1]), jnp.float32)
        for a in range(act):
            recon += jnp.dot(codes_ref[t * act + a], got_ref[ids_ref[t, a]], preferred_element_type=jnp.float32)
        gout = (weight_ref[here, :] * (recon - tok_ref[here, :].astype(jnp.float32))).astype(jnp.bfloat16)
        for a in range(act):
            acc_ref[ids_ref[t, a]] += dot(codes_ref[t * act + a], gout, TN)
            part_ref[t * act + a] = dot(gout, got_ref[ids_ref[t, a]], NT).astype(jnp.bfloat16)
    put(acc_ref, half_ref, grad_ref, out_sem)


def enc_kernel(tb, act, ids_ref, tok_ref, codes_ref, grad_ref, acc_ref):
    sum_rows(tb, act, ids_ref, codes_ref, lambda t: tok_ref[t * BLOCK : (t + 1) * BLOCK, :], acc_ref, grad_ref)


def all_sum(part, axes, n):
    got = lax.all_to_all(part, axes, 0, 0, tiled=True)
    mine = jnp.sum(got.astype(jnp.float32), axis=0).astype(part.dtype)
    return lax.all_to_all(jnp.broadcast_to(mine[None], part.shape), axes, 0, 0, tiled=True)


def per_device(tokens, enc_weight, dec_weight, active_blocks, counts, *, sizes):
    nx, nc, nz, ny = (sizes[k] for k in ("x", "c", "z", "y"))
    nd = nx * nc
    feats = ("x", "c", "y")
    tok_dev, width = tokens.shape
    tb, act = active_blocks.shape
    rows = enc_weight.shape[0]
    lat_blocks = rows * nz * ny // BLOCK
    d = lax.axis_index(("x", "c"))

    swap = [(g * nz + z, z * nz + g) for g in range(nd) for z in range(nz)]
    small = jnp.concatenate([counts, active_blocks.reshape(-1)])
    small = lax.ppermute(small, ("x", "c", "z"), swap)
    weights = small[:tok_dev].astype(jnp.float32)[:, None] / BLOCK
    ids = small[tok_dev:].reshape(tb, act)

    def own_features(weight):
        quarter = [
            lax.dynamic_slice_in_dim(weight, (d * ny + j) * width, width, axis=1) for j in range(ny)
        ]
        got = lax.all_to_all(jnp.stack(quarter), "y", 0, 0, tiled=True)
        return got.reshape(ny * rows, width)

    def all_rows(mine):
        whole = lax.all_gather(mine, "z", axis=0, tiled=True)
        return whole.reshape(lat_blocks, BLOCK, width)

    def own_rows(grad):
        part = lax.psum_scatter(grad.reshape(nz * ny * rows, width), "z", scatter_dimension=0, tiled=True)
        part = lax.all_to_all(part.reshape(ny, rows, width), "y", 0, 0, tiled=True)
        return jnp.concatenate([part[j] for j in range(ny)], axis=1).astype(jnp.float32)

    mine = own_features(enc_weight)
    enc = all_rows(mine)
    tokens, dec_weight, mine = lax.optimization_barrier((tokens, dec_weight, mine))
    dec = all_rows(own_features(dec_weight))
    tok = tokens.reshape(nd, tok_dev // nd, width)
    for axes in (("x", "c"), "z", ("x", "c")):
        tok = lax.all_to_all(tok, axes, 0, 0, tiled=True)
    tok = tok.reshape(tok_dev, width)

    pairs = jax.ShapeDtypeStruct((tb * act, BLOCK, BLOCK), jnp.bfloat16)
    grads = jax.ShapeDtypeStruct((lat_blocks, BLOCK, width), jnp.bfloat16)
    acc = pltpu.VMEM((lat_blocks, BLOCK, width), jnp.float32)

    part = pl.pallas_call(
        functools.partial(pre_kernel, tb, act),
        out_shape=pairs,
        in_specs=[SMEM_SPEC, VMEM_SPEC, VMEM_SPEC],
        out_specs=VMEM_SPEC,
        compiler_params=VMEM,
    )(ids, tok, enc)
    codes = all_sum(part, feats, nd * ny)
    part, group_dec = pl.pallas_call(
        functools.partial(dec_kernel, tb, act),
        out_shape=(pairs, grads),
        in_specs=[SMEM_SPEC] + [VMEM_SPEC] * 3 + [HBM_SPEC],
        out_specs=(VMEM_SPEC, HBM_SPEC),
        scratch_shapes=[acc]
        + [pltpu.VMEM(grads.shape, jnp.bfloat16)] * 2
        + [pltpu.SemaphoreType.DMA, pltpu.SemaphoreType.DMA((PIECES,))],
        compiler_params=VMEM,
    )(ids, tok, weights, codes, dec)
    grad_dec = own_rows(group_dec)
    grad_codes = all_sum(part, feats, nd * ny)
    group_enc = pl.pallas_call(
        functools.partial(enc_kernel, tb, act),
        out_shape=grads,
        in_specs=[SMEM_SPEC] + [VMEM_SPEC] * 2,
        out_specs=VMEM_SPEC,
        scratch_shapes=[acc],
        compiler_params=VMEM,
    )(ids, tok, grad_codes)
    grad_enc = own_rows(group_enc)
    return (grad_enc, grad_dec)


def solution(mesh):
    fine = Mesh(np.asarray(mesh.devices).reshape(4, 2, 8, 4), ("x", "c", "z", "y"))
    dp, latent = ("x", "c"), ("z", "y")
    return jax.shard_map(
        functools.partial(per_device, sizes=dict(fine.shape)),
        mesh=fine,
        in_specs=(P(dp, latent), P(latent, None), P(latent, None), P(dp, None), P(dp)),
        out_specs=(P(latent, dp), P(latent, dp)),
        check_vma=False,
    )
```
